512 devices in a mesh: ky: 64 (over y_lo, z, core), gz: 8 (over y_hi, x).
Axes of the slice: x: 4, y: 8 (y_hi: 2, y_lo: 4; y = y_hi * 4 + y_lo), z: 8, core: 2. Of those that a mesh axis runs over, the one named last changes fastest.
Arguments:
- amplitudes: float32 [2, 512, 1024], P(None, 'ky'), may hold values from -0.046875 to 0.046875
- complementary: float32 [128, 8, 3, 256], P('ky', None, None, 'gz'), may hold values from -6 to 6
Outputs:
- incident: float32 [128, 8, 3, 256], P('ky', None, None, 'gz')
- predicted: float32 [128, 8, 3, 256], P('ky', None, None, 'gz')
The draws below stay inside these ranges and needn't reach their ends.
All inputs are finite; a program needn't handle non-finite values.
Results may differ from the reference program's by a relative error of at most 0.000088.
Values sent between devices are 32-bit elements; how exact they have to be, the bound alone decides.
No kernel may reach another device: no remote copies, remote signals or barrier semaphores. Data moves between devices by JAX's collectives and lax.ppermute only.
A program may use at most 64 MiB of HBM per device.

```python
import jax
import jax.numpy as jnp
from jax import lax

KX = 1024
KY = 512
NX = 128
NY = 256
NZ = 8


def block_levels(key, extent, shards, smallest, largest):
    level, own = 1.0, jax.random.fold_in(key, 6)
    for axis_at, parts in shards:
        heights = jnp.exp(jax.random.uniform(jax.random.fold_in(own, axis_at), (parts,), jnp.float32, smallest / len(shards), largest / len(shards)))
        level = level * jnp.repeat(heights, extent[axis_at] // parts).reshape([-1 if axis == axis_at else 1 for axis in range(len(extent))])
    return level


def scatter_about(key, dims, spread, bound, cuts=(), held_as=jnp.bfloat16):
    array = spread * jax.random.normal(key, dims, jnp.float32)
    if cuts:
        array = array * block_levels(key, dims, cuts, -0.22, 0.18)
    return jnp.clip(array, -bound, bound).astype(held_as)


def setup_inputs(seed: int = 0) -> dict:
    splits = jax.random.split(jax.random.key(seed), 3)
    amplitudes = scatter_about(splits[0], (2, KY, KX), (KX * KY // 32) ** -0.5, 0.046875, ((1, 64),), jnp.float32)
    complementary = scatter_about(splits[1], (NX, NZ, 3, NY), 1.0, 6.0, ((0, 64), (3, 8)), jnp.float32)
    return dict(amplitudes=amplitudes, complementary=complementary)


band_factor = 16.0
cell_height = 0.125
time_step = 0.05
viscosity = 0.02

def incident_block(real_part, imag_part, wave_rows, wave_count, x_points, depths, y_points):
    kx_count = real_part.shape[1]
    along_x = 2.0 * jnp.pi * jnp.arange(kx_count, dtype=jnp.float32) / (band_factor * kx_count)
    along_y = 2.0 * jnp.pi * (wave_rows - wave_count / 2.0) / (band_factor * wave_count)
    magnitude = jnp.sqrt(along_x[None, :] ** 2 + along_y[:, None] ** 2)
    decay_factor = jnp.exp(magnitude[None] * depths[:, None, None])
    scaled_re = decay_factor * real_part[None]
    scaled_im = decay_factor * imag_part[None]
    factor_x = along_x[None, None, :]
    factor_y = along_y[None, :, None]
    factor_k = magnitude[None]
    parts_re = jnp.stack([-factor_x * scaled_im, -factor_y * scaled_im, factor_k * scaled_re], axis=1)
    parts_im = jnp.stack([factor_x * scaled_re, factor_y * scaled_re, factor_k * scaled_im], axis=1)
    stacked = jnp.stack([parts_re, parts_im], axis=2)
    level_count = stacked.shape[0]
    wave_local = stacked.shape[3]
    flat_modes = stacked.reshape(-1, kx_count)
    phase_x = along_x[:, None] * x_points[None, :]
    table_x = jnp.concatenate([jnp.cos(phase_x), jnp.sin(phase_x)], axis=1)
    product = jnp.dot(flat_modes, table_x, precision=lax.Precision.HIGHEST, preferred_element_type=jnp.float32)
    product = product.reshape(level_count, 3, 2, wave_local, 2, x_points.shape[0])
    real_x = product[:, :, 0, :, 0] - product[:, :, 1, :, 1]
    imag_x = product[:, :, 0, :, 1] + product[:, :, 1, :, 0]
    combined = jnp.concatenate([real_x, -imag_x], axis=2)
    phase_y = along_y[:, None] * y_points[None, :]
    table_y = jnp.concatenate([jnp.cos(phase_y), jnp.sin(phase_y)], axis=0)
    return jnp.einsum('lcnx,ny->xlcy', combined, table_y, precision=lax.Precision.HIGHEST)

def trimmed(array_in, axis_cut, first_index, index_count):
    result = array_in
    for other_axis in (0, 1, 3):
        if other_axis == axis_cut:
            result = lax.slice_in_dim(result, first_index, first_index + index_count, axis=other_axis)
        else:
            result = lax.slice_in_dim(result, 1, result.shape[other_axis] - 1, axis=other_axis)
    return result

def predict(padded):
    expanded = jnp.pad(padded, ((0, 0), (1, 1), (0, 0), (0, 0)))
    centre_uc = trimmed(expanded, 1, 1, expanded.shape[1] - 2)[:, :, 3:]
    tendency = jnp.zeros_like(centre_uc)
    for spatial, normal, spacing in ((0, 0, 1.0), (3, 1, 1.0), (1, 2, cell_height)):
        inner_count = expanded.shape[spatial] - 2
        lower_cells = trimmed(expanded, spatial, 0, inner_count + 1)
        upper_cells = trimmed(expanded, spatial, 1, inner_count + 1)
        face_values = 0.5 * (lower_cells + upper_cells)
        face_inc = face_values[:, :, :3]
        face_comp = face_values[:, :, 3:]
        normal_total = face_inc[:, :, normal] + face_comp[:, :, normal]
        face_flux = normal_total[:, :, None] * face_comp + face_comp[:, :, normal][:, :, None] * face_inc
        divergence = (lax.slice_in_dim(face_flux, 1, inner_count + 1, axis=spatial) - lax.slice_in_dim(face_flux, 0, inner_count, axis=spatial)) / spacing
        neighbours = trimmed(expanded, spatial, 0, inner_count)[:, :, 3:] + trimmed(expanded, spatial, 2, inner_count)[:, :, 3:]
        tendency = tendency - divergence + viscosity * (neighbours - 2.0 * centre_uc) / (spacing * spacing)
    return centre_uc + time_step * tendency

def reference(amplitudes, complementary):
    wave_count = amplitudes.shape[1]
    wave_rows = jnp.arange(wave_count, dtype=jnp.float32)
    x_points = jnp.arange(NX, dtype=jnp.float32) + 0.5
    y_points = jnp.arange(NY, dtype=jnp.float32) + 0.5

    def one_level(level_index):
        level_depth = -(level_index.astype(jnp.float32) + 0.5) * cell_height
        return incident_block(amplitudes[0], amplitudes[1], wave_rows, wave_count, x_points, level_depth[None], y_points)[:, 0]
    levels_first = lax.map(one_level, jnp.arange(NZ, dtype=jnp.int32))
    incident = jnp.transpose(levels_first, (1, 0, 2, 3))
    stacked = jnp.concatenate([incident, complementary], axis=2)
    padded = jnp.pad(stacked, ((1, 1), (0, 0), (0, 0), (1, 1)))
    return (incident, predict(padded))
```

```python
import jax
import jax.numpy as jnp
import ml_dtypes
import numpy as np
from jax import lax
from jax.experimental import pallas as pl
from jax.experimental.pallas import tpu as pltpu
from jax.sharding import PartitionSpec as P

band_factor = 16.0
cell_height = 0.125
time_step = 0.05
viscosity = 0.02
lanes = 128
f32 = jnp.float32


def split(x):
    high = x.astype(jnp.bfloat16)
    return high, (x - high.astype(f32)).astype(jnp.bfloat16)


def split_table(table):
    high = table.astype(np.float32).astype(ml_dtypes.bfloat16)
    return high, (table - high.astype(np.float64)).astype(np.float32).astype(ml_dtypes.bfloat16)


def x_tables(kx_count, zone_x, x_tile):
    cells = np.arange(zone_x).reshape(-1, x_tile).T.reshape(-1)
    turns = np.outer(cells * 2 + 1, np.arange(kx_count)) % int(2 * band_factor * kx_count)
    phase = turns * (2.0 * np.pi / (2 * band_factor * kx_count))
    return split_table(np.concatenate([np.cos(phase), np.sin(phase)], axis=0))


def y_tables(wave_count, zone_y, y_tile, wave_local, height):
    tiles = zone_y // y_tile
    cells = np.arange(tiles)[:, None] * y_tile + np.arange(y_tile + 2)[None] - 1
    inside = (cells >= 0) & (cells < zone_y)
    rows = np.arange(wave_count).reshape(-1, wave_local).T.reshape(-1) - wave_count // 2
    turns = (cells[..., None] * 2 + 1) * rows % int(2 * band_factor * wave_count)
    phase = turns * (2.0 * np.pi / (2 * band_factor * wave_count))
    table = np.concatenate([np.cos(phase), -np.sin(phase)], axis=-1) * inside[..., None]
    table = np.pad(table, ((0, 0), (0, height - table.shape[1]), (0, 0)))
    return np.concatenate(split_table(table), axis=1)


def dot_nt(a, b):
    return lax.dot_general(a, b, (((1,), (1,)), ((), ())), preferred_element_type=f32)


def x_kernel(ky_groups, level_count, wave_count, amplitudes, table_hi, table_lo, out):
    wave_local, kx_count = amplitudes.shape[1:]
    per_row = 3 * level_count
    first = lax.axis_index("ky") * wave_local
    rows = (first + lax.broadcasted_iota(jnp.int32, (wave_local, kx_count), 0)).astype(f32)
    step_y = 2.0 * np.pi / (band_factor * wave_count)
    step_x = 2.0 * np.pi / (band_factor * kx_count)
    along_y = (rows - wave_count / 2.0) * step_y
    columns = lax.broadcasted_iota(jnp.int32, (wave_local, kx_count), 1).astype(f32)
    along_x = columns * step_x
    magnitude = jnp.sqrt(along_x * along_x + along_y * along_y)
    shape = (level_count, kx_count)
    depths = -(lax.broadcasted_iota(jnp.int32, shape, 0).astype(f32) + 0.5) * cell_height
    kx = along_x[0:1]
    parts_re, parts_im = [], []
    for n in range(wave_local):
        k = magnitude[n : n + 1]
        ky = along_y[n : n + 1]
        decay = jnp.exp(jnp.broadcast_to(k, shape) * depths)
        re = decay * amplitudes[0, n : n + 1]
        im = decay * amplitudes[1, n : n + 1]
        parts_re += [-kx * im, -ky * im, k * re]
        parts_im += [kx * re, ky * re, k * im]
    modes_hi, modes_lo = split(jnp.concatenate(parts_re + parts_im, axis=0))
    product = dot_nt(table_hi[...], modes_hi)
    product += dot_nt(table_hi[...], modes_lo) + dot_nt(table_lo[...], modes_hi)
    half = product.shape[0] // 2
    by_cos, by_sin = product[:half], product[half:]
    middle = wave_local * per_row
    turned = jnp.concatenate([-by_sin[:, middle:], by_sin[:, :middle]], axis=1)
    field = by_cos + turned
    even, odd = field[:ky_groups], field[ky_groups:]
    width = field.shape[1] // lanes
    chunk = 4 * width
    for j in range(width):
        cut = slice(lanes * j, lanes * (j + 1))
        out[pl.ds(j + chunk, ky_groups - 1, stride=chunk), :] = odd[: ky_groups - 1, cut]
        out[pl.ds(j, 1), :] = jnp.zeros((1, lanes), f32)
        out[pl.ds(j + width, ky_groups, stride=chunk), :] = even[:, cut]
        out[pl.ds(j + 2 * width, ky_groups, stride=chunk), :] = odd[:, cut]
        out[pl.ds(j + 3 * width, ky_groups - 1, stride=chunk), :] = even[1:, cut]
        out[pl.ds((ky_groups - 1) * chunk + j + 3 * width, 1), :] = jnp.zeros((1, lanes), f32)


def face(a, b):
    return [0.5 * (p + q) for p, q in zip(a, b)]


def flux(inc, comp, normal):
    total = inc[normal] + comp[normal]
    return [total * comp[c] + comp[normal] * inc[c] for c in range(3)]


def y_kernel(ky_groups, wave_local, height, received, table, comp, x_low, x_high, y_low, y_high, incident, predicted, padded):
    level_count, y_tile = comp.shape[2:]
    per_row = 3 * level_count
    width = 2 * wave_local * per_row // lanes
    chunk = 4 * width
    cols = [[received[pl.ds(k * width + t, ky_groups, stride=chunk), :] for t in range(width)] for k in range(4)]
    lane = lax.broadcasted_iota(jnp.int32, (ky_groups, lanes), 1)
    blocks = []
    for b in range(2 * wave_local):
        first, offset = divmod(b * per_row, lanes)
        block = None
        for k in range(4):
            at = k * per_row
            shift = (at - offset) % lanes
            piece = pltpu.roll(cols[k][first], shift, axis=1) if shift else cols[k][first]
            if offset + per_row > lanes:
                rest = pltpu.roll(cols[k][first + 1], shift, axis=1) if shift else cols[k][first + 1]
                piece = jnp.where(lane < at + lanes - offset, piece, rest)
            block = piece if block is None else jnp.where(lane < at, block, piece)
        blocks.append(block)
    modes_hi, modes_lo = split(jnp.concatenate(blocks, axis=0))
    both = jnp.dot(table[...], modes_hi, preferred_element_type=f32)
    field = both[:height] + both[height:]
    field += jnp.dot(table[:height], modes_lo, preferred_element_type=f32)
    field = jnp.concatenate([field, jnp.zeros((lanes - height, lanes), f32)], axis=0).T
    inc = [
        [field[(k * 3 + c) * level_count : (k * 3 + c + 1) * level_count] for c in range(3)]
        for k in range(4)
    ]
    padded[...] = jnp.zeros_like(padded)
    for c in range(3):
        padded[0, c, :, 1 : y_tile + 1] = x_low[1, c]
        padded[3, c, :, 1 : y_tile + 1] = x_high[0, c]
        for x in range(2):
            padded[x + 1, c, :, 1 : y_tile + 1] = comp[x, c]
            padded[x + 1, c, :, 0:1] = y_low[x, c, :, y_tile - 1 : y_tile]
            padded[x + 1, c, :, y_tile + 1 : y_tile + 2] = y_high[x, c, :, 0:1]
    cells = [[padded[k, c] for c in range(3)] for k in range(4)]
    level = lax.broadcasted_iota(jnp.int32, (level_count, lanes), 0)

    def below(v):
        return jnp.where(level == 0, 0.0, pltpu.roll(v, 1, axis=0))

    def above(v):
        return jnp.where(level == level_count - 1, 0.0, pltpu.roll(v, level_count - 1, axis=0))

    def before(v):
        return pltpu.roll(v, 1, axis=1)

    def after(v):
        return pltpu.roll(v, lanes - 1, axis=1)

    x_flux = [flux(face(inc[k], inc[k + 1]), face(cells[k], cells[k + 1]), 0) for k in range(3)]
    for x in range(2):
        own_inc, own = inc[x + 1], cells[x + 1]
        inc_before, own_before = [before(v) for v in own_inc], [before(v) for v in own]
        y_lower = flux(face(inc_before, own_inc), face(own_before, own), 1)
        inc_below, own_below = [below(v) for v in own_inc], [below(v) for v in own]
        inc_above, own_above = [above(v) for v in own_inc], [above(v) for v in own]
        z_lower = flux(face(inc_below, own_inc), face(own_below, own), 2)
        z_upper = flux(face(own_inc, inc_above), face(own, own_above), 2)
        for c in range(3):
            twice = 2.0 * own[c]
            tendency = -(x_flux[x + 1][c] - x_flux[x][c])
            tendency += viscosity * (cells[x][c] + cells[x + 2][c] - twice)
            tendency -= after(y_lower[c]) - y_lower[c]
            tendency += viscosity * (own_before[c] + after(own[c]) - twice)
            tendency -= (z_upper[c] - z_lower[c]) / cell_height
            tendency += viscosity * (own_below[c] + own_above[c] - twice) / cell_height**2
            result = own[c] + time_step * tendency
            incident[x, c] = own_inc[c][:, 1 : y_tile + 1]
            predicted[x, c] = result[:, 1 : y_tile + 1]


def on_device(amplitudes, complementary):
    x_tile, level_count, _, y_tile = complementary.shape
    ky_groups, gz_groups = lax.axis_size("ky"), lax.axis_size("gz")
    wave_local, kx_count = amplitudes.shape[1:]
    wave_count = wave_local * ky_groups
    height = -(-(y_tile + 2) // 8) * 8
    chunk = 4 * 2 * wave_local * 3 * level_count // lanes
    table_hi, table_lo = x_tables(kx_count, x_tile * ky_groups, x_tile)
    table_y = y_tables(wave_count, y_tile * gz_groups, y_tile, wave_local, height)
    vmem = pl.BlockSpec(memory_space=pltpu.VMEM)

    def x_call(*refs):
        x_kernel(ky_groups, level_count, wave_count, *refs)

    def y_call(*refs):
        y_kernel(ky_groups, wave_local, height, *refs)

    with jax.named_scope("x_transform"):
        sent = pl.pallas_call(
            x_call,
            out_shape=jax.ShapeDtypeStruct((ky_groups * chunk, lanes), f32),
            in_specs=[vmem] * 3,
            out_specs=vmem,
            compiler_params=pltpu.CompilerParams(vmem_limit_bytes=48 * 2**20),
            name="x_transform",
        )(amplitudes, jnp.asarray(table_hi), jnp.asarray(table_lo))
    comp = jnp.transpose(complementary, (0, 2, 1, 3))
    halos = []
    for axis, size in (("ky", ky_groups), ("gz", gz_groups)):
        up = [(i, i + 1) for i in range(size - 1)]
        halos.append(lax.ppermute(comp, axis, up))
        halos.append(lax.ppermute(comp, axis, [(j, i) for i, j in up]))
    received = lax.all_to_all(sent.reshape(ky_groups, chunk, lanes), "ky", 0, 0)
    table = lax.dynamic_index_in_dim(jnp.asarray(table_y), lax.axis_index("gz"), 0, keepdims=False)
    result = jax.ShapeDtypeStruct(comp.shape, f32)
    with jax.named_scope("y_transform_and_step"):
        incident, predicted = pl.pallas_call(
            y_call,
            out_shape=(result, result),
            in_specs=[vmem] * 7,
            out_specs=(vmem, vmem),
            scratch_shapes=[pltpu.VMEM((4, 3, level_count, lanes), f32)],
            compiler_params=pltpu.CompilerParams(vmem_limit_bytes=48 * 2**20),
            name="y_transform",
        )(received.reshape(ky_groups * chunk, lanes), table, comp, *halos)
    back = (0, 2, 1, 3)
    return jnp.transpose(incident, back), jnp.transpose(predicted, back)


def solution(mesh):
    placed = (P(None, "ky", None), P("ky", None, None, "gz"))
    return jax.shard_map(
        on_device,
        mesh=mesh,
        in_specs=placed,
        out_specs=(P("ky", None, None, "gz"), P("ky", None, None, "gz")),
        check_vma=False,
    )
```

```python
import jax
import jax.numpy as jnp
import ml_dtypes
import numpy as np
from jax import lax
from jax.experimental import pallas as pl
from jax.experimental.pallas import tpu as pltpu
from jax.sharding import PartitionSpec as P

band_factor = 16.0
cell_height = 0.125
time_step = 0.05
viscosity = 0.02
lanes = 128
f32 = jnp.float32


def split(x):
    high = x.astype(jnp.bfloat16)
    return high, (x - high.astype(f32)).astype(jnp.bfloat16)


def split_table(table):
    high = table.astype(np.float32).astype(ml_dtypes.bfloat16)
    return high, (table - high.astype(np.float64)).astype(np.float32).astype(ml_dtypes.bfloat16)


def x_tables(kx_count):
    near = np.arange(16).reshape(8, 2).T.reshape(-1) * 2 + 1
    halves = np.concatenate([near, 32 * np.arange(8)])
    turns = np.outer(halves, np.arange(kx_count)) % int(2 * band_factor * kx_count)
    phase = turns * (2.0 * np.pi / (2 * band_factor * kx_count))
    return np.stack([np.cos(phase), np.sin(phase)]).astype(np.float32)


def y_tables(wave_count, zone_y, y_tile, wave_local, height):
    tiles = zone_y // y_tile
    cells = np.arange(tiles)[:, None] * y_tile + np.arange(y_tile + 2)[None] - 1
    inside = (cells >= 0) & (cells < zone_y)
    rows = np.arange(wave_count).reshape(-1, wave_local).T.reshape(-1) - wave_count // 2
    turns = (cells[..., None] * 2 + 1) * rows % int(2 * band_factor * wave_count)
    phase = turns * (2.0 * np.pi / (2 * band_factor * wave_count))
    table = np.concatenate([np.cos(phase), -np.sin(phase)], axis=-1) * inside[..., None]
    table = np.pad(table, ((0, 0), (0, height - table.shape[1]), (0, 0)))
    return np.concatenate(split_table(table), axis=1)


def dot_nt(a, b):
    return lax.dot_general(a, b, (((1,), (1,)), ((), ())), preferred_element_type=f32)


def x_kernel(ky_groups, level_count, wave_count, amplitudes, tables, out, modes, table, sems):
    copies = [
        pltpu.make_async_copy(source, target, sems.at[i])
        for i, (source, target) in enumerate(((tables, table), (amplitudes, modes)))
    ]
    for copy in copies:
        copy.start()
    wave_local, kx_count = amplitudes.shape[1:]
    per_row = 3 * level_count
    me = lax.axis_index("ky")
    rows = (me * wave_local + lax.broadcasted_iota(jnp.int32, (wave_local, kx_count), 0)).astype(f32)
    step_y = 2.0 * np.pi / (band_factor * wave_count)
    step_x = 2.0 * np.pi / (band_factor * kx_count)
    along_y = (rows - wave_count / 2.0) * step_y
    columns = lax.broadcasted_iota(jnp.int32, (wave_local, kx_count), 1).astype(f32)
    along_x = columns * step_x
    magnitude = jnp.sqrt(along_x * along_x + along_y * along_y)
    shape = (level_count, kx_count)
    depths = -(lax.broadcasted_iota(jnp.int32, shape, 0).astype(f32) + 0.5) * cell_height
    kx = along_x[0:1]
    decays = [jnp.exp(jnp.broadcast_to(magnitude[n : n + 1], shape) * depths) for n in range(wave_local)]
    copies[0].wait()
    cos_rows, sin_rows = [], []
    for e in range(2):
        cos_near, sin_near = table[0, 8 * e : 8 * e + 8], table[1, 8 * e : 8 * e + 8]
        for i in range(ky_groups // 8):
            cos_far, sin_far = table[0, 16 + i : 17 + i], table[1, 16 + i : 17 + i]
            cos_rows.append(cos_near * cos_far - sin_near * sin_far)
            sin_rows.append(sin_near * cos_far + cos_near * sin_far)
    table_hi, table_lo = split(jnp.concatenate(cos_rows + sin_rows, axis=0))
    copies[1].wait()
    parts_re, parts_im = [], []
    for n in range(wave_local):
        k = magnitude[n : n + 1]
        ky = along_y[n : n + 1]
        re = decays[n] * modes[0, n : n + 1]
        im = decays[n] * modes[1, n : n + 1]
        parts_re += [-kx * im, -ky * im, k * re]
        parts_im += [kx * re, ky * re, k * im]
    modes_hi, modes_lo = split(jnp.concatenate(parts_re + parts_im, axis=0))
    product = dot_nt(table_hi, modes_hi)
    product += dot_nt(table_hi, modes_lo) + dot_nt(table_lo, modes_hi)
    half = product.shape[0] // 2
    by_cos, by_sin = product[:half], product[half:]
    middle = wave_local * per_row
    turned = jnp.concatenate([-by_sin[:, middle:], by_sin[:, :middle]], axis=1)
    field = by_cos + turned
    even, odd = field[:ky_groups], field[ky_groups:]
    width = field.shape[1] // lanes
    chunk = 4 * width
    for j in range(width):
        cut = slice(lanes * j, lanes * (j + 1))
        out[pl.ds(j + chunk, ky_groups - 1, stride=chunk), :] = odd[: ky_groups - 1, cut]
        out[pl.ds(j, 1), :] = jnp.zeros((1, lanes), f32)
        out[pl.ds(j + width, ky_groups, stride=chunk), :] = even[:, cut]
        out[pl.ds(j + 2 * width, ky_groups, stride=chunk), :] = odd[:, cut]
        out[pl.ds(j + 3 * width, ky_groups - 1, stride=chunk), :] = even[1:, cut]
        out[pl.ds((ky_groups - 1) * chunk + j + 3 * width, 1), :] = jnp.zeros((1, lanes), f32)


def face(a, b):
    return [0.5 * (p + q) for p, q in zip(a, b)]


def flux(inc, comp, normal):
    total = inc[normal] + comp[normal]
    return [total * comp[c] + comp[normal] * inc[c] for c in range(3)]


def y_kernel(ky_groups, wave_local, height, received, table, comp, y_out, y_in, x_out, x_in, incident, predicted, padded):
    per_row, y_tile = comp.shape[1:]
    level_count = per_row // 3
    width = 2 * wave_local * per_row // lanes
    chunk = 4 * width
    cols = [[received[pl.ds(k * width + t, ky_groups, stride=chunk), :] for t in range(width)] for k in range(4)]
    lane = lax.broadcasted_iota(jnp.int32, (ky_groups, lanes), 1)
    blocks = []
    for b in range(2 * wave_local):
        first, offset = divmod(b * per_row, lanes)
        block = None
        for k in range(4):
            at = k * per_row
            shift = (at - offset) % lanes
            piece = pltpu.roll(cols[k][first], shift, axis=1) if shift else cols[k][first]
            if offset + per_row > lanes:
                rest = pltpu.roll(cols[k][first + 1], shift, axis=1) if shift else cols[k][first + 1]
                piece = jnp.where(lane < at + lanes - offset, piece, rest)
            block = piece if block is None else jnp.where(lane < at, block, piece)
        blocks.append(block)
    modes_hi, modes_lo = split(jnp.concatenate(blocks, axis=0))
    both = jnp.dot(table[...], modes_hi, preferred_element_type=f32)
    field = both[:height] + both[height:]
    field += jnp.dot(table[:height], modes_lo, preferred_element_type=f32)
    field = jnp.concatenate([field, jnp.zeros((lanes - height, lanes), f32)], axis=0).T
    inc = [
        [field[(k * 3 + c) * level_count : (k * 3 + c + 1) * level_count] for c in range(3)]
        for k in range(4)
    ]
    padded[...] = jnp.zeros_like(padded)
    x_even = lax.axis_index("ky") % 2 == 0
    y_even = lax.axis_index("gz") % 2 == 0
    inner = slice(1, y_tile + 1)
    padded[0, :, inner] = jnp.where(x_even, x_out[1], x_in[1])
    padded[3, :, inner] = jnp.where(x_even, x_in[0], x_out[0])
    for x in range(2):
        padded[x + 1, :, inner] = comp[x]
        padded[x + 1, :, 0:1] = jnp.where(y_even, y_out[x], y_in[x])[:, y_tile - 1 : y_tile]
        padded[x + 1, :, y_tile + 1 : y_tile + 2] = jnp.where(y_even, y_in[x], y_out[x])[:, 0:1]
    cells = [[padded[k, c * level_count : (c + 1) * level_count] for c in range(3)] for k in range(4)]
    level = lax.broadcasted_iota(jnp.int32, (level_count, lanes), 0)

    def below(v):
        return jnp.where(level == 0, 0.0, pltpu.roll(v, 1, axis=0))

    def above(v):
        return jnp.where(level == level_count - 1, 0.0, pltpu.roll(v, level_count - 1, axis=0))

    def before(v):
        return pltpu.roll(v, 1, axis=1)

    def after(v):
        return pltpu.roll(v, lanes - 1, axis=1)

    x_flux = [flux(face(inc[k], inc[k + 1]), face(cells[k], cells[k + 1]), 0) for k in range(3)]
    for x in range(2):
        own_inc, own = inc[x + 1], cells[x + 1]
        inc_before, own_before = [before(v) for v in own_inc], [before(v) for v in own]
        y_lower = flux(face(inc_before, own_inc), face(own_before, own), 1)
        inc_below, own_below = [below(v) for v in own_inc], [below(v) for v in own]
        inc_above, own_above = [above(v) for v in own_inc], [above(v) for v in own]
        z_lower = flux(face(inc_below, own_inc), face(own_below, own), 2)
        z_upper = flux(face(own_inc, inc_above), face(own, own_above), 2)
        for c in range(3):
            twice = 2.0 * own[c]
            tendency = -(x_flux[x + 1][c] - x_flux[x][c])
            tendency += viscosity * (cells[x][c] + cells[x + 2][c] - twice)
            tendency -= after(y_lower[c]) - y_lower[c]
            tendency += viscosity * (own_before[c] + after(own[c]) - twice)
            tendency -= (z_upper[c] - z_lower[c]) / cell_height
            tendency += viscosity * (own_below[c] + own_above[c] - twice) / cell_height**2
            result = own[c] + time_step * tendency
            incident[x, c] = own_inc[c][:, 1 : y_tile + 1]
            predicted[x, c] = result[:, 1 : y_tile + 1]


def swaps(size, first):
    pairs = [(i, i + 1) for i in range(first, size - 1, 2)]
    return pairs + [(j, i) for i, j in pairs]


PAIRS = (("ky", 0), ("ky", 1), ("gz", 0), ("gz", 1))
ORDER = (("gz", 1), ("gz", 0), ("ky", 1), ("ky", 0))


def on_device(amplitudes, complementary):
    x_tile, level_count, _, y_tile = complementary.shape
    ky_groups, gz_groups = lax.axis_size("ky"), lax.axis_size("gz")
    wave_local, kx_count = amplitudes.shape[1:]
    wave_count = wave_local * ky_groups
    height = -(-(y_tile + 2) // 8) * 8
    chunk = 4 * 2 * wave_local * 3 * level_count // lanes
    table_x = x_tables(kx_count)
    table_y = y_tables(wave_count, y_tile * gz_groups, y_tile, wave_local, height)
    vmem = pl.BlockSpec(memory_space=pltpu.VMEM)
    anywhere = pl.BlockSpec(memory_space=pl.ANY)

    def x_call(*refs):
        x_kernel(ky_groups, level_count, wave_count, *refs)

    def y_call(*refs):
        y_kernel(ky_groups, wave_local, height, *refs)

    comp = jnp.transpose(complementary, (0, 2, 1, 3)).reshape(x_tile, 3 * level_count, y_tile)
    with jax.named_scope("x_transform"):
        sent = pl.pallas_call(
            x_call,
            out_shape=jax.ShapeDtypeStruct((ky_groups * chunk, lanes), f32),
            in_specs=[anywhere] * 2,
            out_specs=vmem,
            scratch_shapes=[
                pltpu.VMEM(amplitudes.shape, f32),
                pltpu.VMEM(table_x.shape, f32),
                pltpu.SemaphoreType.DMA((2,)),
            ],
            name="x_transform",
        )(amplitudes, jnp.asarray(table_x))
    halos = [
        lax.ppermute(comp, axis, swaps(lax.axis_size(axis), first)) for axis, first in ORDER
    ]
    x_in, x_out, y_in, y_out = (halos[ORDER.index(which)] for which in PAIRS)
    received = lax.all_to_all(sent.reshape(ky_groups, 1, chunk * lanes), "ky", 0, 0)
    table = lax.dynamic_index_in_dim(jnp.asarray(table_y), lax.axis_index("gz"), 0, keepdims=False)
    result = jax.ShapeDtypeStruct((x_tile, 3, level_count, y_tile), f32)
    with jax.named_scope("y_transform_and_step"):
        incident, predicted = pl.pallas_call(
            y_call,
            out_shape=(result, result),
            in_specs=[vmem] * 7,
            out_specs=(vmem, vmem),
            scratch_shapes=[pltpu.VMEM((4, 3 * level_count, lanes), f32)],
            compiler_params=pltpu.CompilerParams(vmem_limit_bytes=48 * 2**20),
            name="y_transform",
        )(received.reshape(ky_groups * chunk, lanes), table, comp, y_out, y_in, x_out, x_in)
    back = (0, 2, 1, 3)
    return jnp.transpose(incident, back), jnp.transpose(predicted, back)


def solution(mesh):
    placed = (P(None, "ky", None), P("ky", None, None, "gz"))
    return jax.shard_map(
        on_device,
        mesh=mesh,
        in_specs=placed,
        out_specs=(P("ky", None, None, "gz"), P("ky", None, None, "gz")),
        check_vma=False,
    )
```

```python
import jax
import jax.numpy as jnp
import numpy as np
from jax import lax
from jax.experimental import pallas as pl
from jax.experimental.pallas import tpu as pltpu
from jax.sharding import PartitionSpec as P

band_factor = 16.0
cell_height = 0.125
time_step = 0.05
viscosity = 0.02
lanes = 128
f32 = jnp.float32


def split(x):
    high = x.astype(jnp.bfloat16)
    return high, (x - high.astype(f32)).astype(jnp.bfloat16)


def cos_sin(turns, period):
    quarter = period // 4
    turns = turns & (period - 1)
    which = ((turns + quarter // 2) // quarter) & 3
    angle = (turns - (turns + quarter // 2) // quarter * quarter).astype(f32) * (2.0 * np.pi / period)
    square = angle * angle
    sin, cos = jnp.full_like(square, 1.0), jnp.full_like(square, 1.0)
    for n in (8, 6, 4, 2):
        sin = 1.0 - sin * square * (1.0 / (n * (n + 1)))
    for n in (9, 7, 5, 3, 1):
        cos = 1.0 - cos * square * (1.0 / (n * (n + 1)))
    sin = sin * angle
    swapped = (which & 1) == 1
    first, second = jnp.where(swapped, sin, cos), jnp.where(swapped, cos, sin)
    return (
        jnp.where((which == 1) | (which == 2), -first, first),
        jnp.where(which >= 2, -second, second),
    )


def x_tables(ky_groups, kx_count):
    period = int(2 * band_factor * kx_count)
    row = lax.broadcasted_iota(jnp.int32, (24, kx_count), 0)
    halves = jnp.where(row < 16, row % 8 * 4 + row // 8 * 2 + 1, 32 * (row - 16))
    cos, sin = cos_sin(halves * lax.broadcasted_iota(jnp.int32, (24, kx_count), 1), period)
    cos_rows, sin_rows = [], []
    for e in range(2):
        near = slice(8 * e, 8 * e + 8)
        for i in range(ky_groups // 8):
            far = slice(16 + i, 17 + i)
            cos_rows.append(cos[near] * cos[far] - sin[near] * sin[far])
            sin_rows.append(sin[near] * cos[far] + cos[near] * sin[far])
    return jnp.concatenate(cos_rows + sin_rows, axis=0)


def y_tables(y_tile, ky_groups, wave_local, height):
    wave_count = ky_groups * wave_local
    shape = (height, wave_count)
    row, column = (lax.broadcasted_iota(jnp.int32, shape, axis) for axis in (0, 1))
    cell = lax.axis_index("gz") * y_tile + row - 1
    inside = (cell >= 0) & (cell < lax.axis_size("gz") * y_tile) & (row < y_tile + 2)
    wave = column % ky_groups * wave_local + column // ky_groups - wave_count // 2
    cos, sin = cos_sin((2 * cell + 1) * wave, int(2 * band_factor * wave_count))
    return jnp.concatenate([jnp.where(inside, cos, 0.0), jnp.where(inside, -sin, 0.0)], axis=1)


def dot_nt(a, b):
    return lax.dot_general(a, b, (((1,), (1,)), ((), ())), preferred_element_type=f32)


def x_kernel(ky_groups, level_count, wave_count, amplitudes, out, modes, sem):
    copy = pltpu.make_async_copy(amplitudes, modes, sem)
    copy.start()
    wave_local, kx_count = amplitudes.shape[1:]
    per_row = 3 * level_count
    me = lax.axis_index("ky")
    rows = (me * wave_local + lax.broadcasted_iota(jnp.int32, (wave_local, kx_count), 0)).astype(f32)
    step_y = 2.0 * np.pi / (band_factor * wave_count)
    step_x = 2.0 * np.pi / (band_factor * kx_count)
    along_y = (rows - wave_count / 2.0) * step_y
    columns = lax.broadcasted_iota(jnp.int32, (wave_local, kx_count), 1).astype(f32)
    along_x = columns * step_x
    magnitude = jnp.sqrt(along_x * along_x + along_y * along_y)
    shape = (level_count, kx_count)
    depths = -(lax.broadcasted_iota(jnp.int32, shape, 0).astype(f32) + 0.5) * cell_height
    kx = along_x[0:1]
    decays = [jnp.exp(jnp.broadcast_to(magnitude[n : n + 1], shape) * depths) for n in range(wave_local)]
    table_hi, table_lo = split(x_tables(ky_groups, kx_count))
    copy.wait()
    parts_re, parts_im = [], []
    for n in range(wave_local):
        k = magnitude[n : n + 1]
        ky = along_y[n : n + 1]
        re = decays[n] * modes[0, n : n + 1]
        im = decays[n] * modes[1, n : n + 1]
        parts_re += [-kx * im, -ky * im, k * re]
        parts_im += [kx * re, ky * re, k * im]
    modes_hi, modes_lo = split(jnp.concatenate(parts_re + parts_im, axis=0))
    product = dot_nt(table_hi, modes_hi)
    product += dot_nt(table_hi, modes_lo) + dot_nt(table_lo, modes_hi)
    half = product.shape[0] // 2
    by_cos, by_sin = product[:half], product[half:]
    middle = wave_local * per_row
    turned = jnp.concatenate([-by_sin[:, middle:], by_sin[:, :middle]], axis=1)
    field = by_cos + turned
    even, odd = field[:ky_groups], field[ky_groups:]
    width = field.shape[1] // lanes
    chunk = 4 * width
    for j in range(width):
        cut = slice(lanes * j, lanes * (j + 1))
        out[pl.ds(j + chunk, ky_groups - 1, stride=chunk), :] = odd[: ky_groups - 1, cut]
        out[pl.ds(j, 1), :] = jnp.zeros((1, lanes), f32)
        out[pl.ds(j + width, ky_groups, stride=chunk), :] = even[:, cut]
        out[pl.ds(j + 2 * width, ky_groups, stride=chunk), :] = odd[:, cut]
        out[pl.ds(j + 3 * width, ky_groups - 1, stride=chunk), :] = even[1:, cut]
        out[pl.ds((ky_groups - 1) * chunk + j + 3 * width, 1), :] = jnp.zeros((1, lanes), f32)


def face(a, b):
    return [0.5 * (p + q) for p, q in zip(a, b)]


def flux(inc, comp, normal):
    total = inc[normal] + comp[normal]
    return [total * comp[c] + comp[normal] * inc[c] for c in range(3)]


def y_kernel(ky_groups, wave_local, height, received, comp, y_out, y_in, x_out, x_in, incident, predicted, padded):
    per_row, y_tile = comp.shape[1:]
    level_count = per_row // 3
    width = 2 * wave_local * per_row // lanes
    chunk = 4 * width
    cols = [[received[pl.ds(k * width + t, ky_groups, stride=chunk), :] for t in range(width)] for k in range(4)]
    lane = lax.broadcasted_iota(jnp.int32, (ky_groups, lanes), 1)
    blocks = []
    for b in range(2 * wave_local):
        first, offset = divmod(b * per_row, lanes)
        block = None
        for k in range(4):
            at = k * per_row
            shift = (at - offset) % lanes
            piece = pltpu.roll(cols[k][first], shift, axis=1) if shift else cols[k][first]
            if offset + per_row > lanes:
                rest = pltpu.roll(cols[k][first + 1], shift, axis=1) if shift else cols[k][first + 1]
                piece = jnp.where(lane < at + lanes - offset, piece, rest)
            block = piece if block is None else jnp.where(lane < at, block, piece)
        blocks.append(block)
    modes_hi, modes_lo = split(jnp.concatenate(blocks, axis=0))
    table_hi, table_lo = split(y_tables(y_tile, ky_groups, wave_local, height))
    both = jnp.dot(jnp.concatenate([table_hi, table_lo], axis=0), modes_hi, preferred_element_type=f32)
    field = both[:height] + both[height:]
    field += jnp.dot(table_hi, modes_lo, preferred_element_type=f32)
    field = jnp.concatenate([field, jnp.zeros((lanes - height, lanes), f32)], axis=0).T
    inc = [
        [field[(k * 3 + c) * level_count : (k * 3 + c + 1) * level_count] for c in range(3)]
        for k in range(4)
    ]
    padded[...] = jnp.zeros_like(padded)
    x_even = lax.axis_index("ky") % 2 == 0
    y_even = lax.axis_index("gz") % 2 == 0
    inner = slice(1, y_tile + 1)
    padded[0, :, inner] = jnp.where(x_even, x_out[1], x_in[1])
    padded[3, :, inner] = jnp.where(x_even, x_in[0], x_out[0])
    for x in range(2):
        padded[x + 1, :, inner] = comp[x]
        padded[x + 1, :, 0:1] = jnp.where(y_even, y_out[x], y_in[x])[:, y_tile - 1 : y_tile]
        padded[x + 1, :, y_tile + 1 : y_tile + 2] = jnp.where(y_even, y_in[x], y_out[x])[:, 0:1]
    cells = [[padded[k, c * level_count : (c + 1) * level_count] for c in range(3)] for k in range(4)]
    level = lax.broadcasted_iota(jnp.int32, (level_count, lanes), 0)

    def below(v):
        return jnp.where(level == 0, 0.0, pltpu.roll(v, 1, axis=0))

    def above(v):
        return jnp.where(level == level_count - 1, 0.0, pltpu.roll(v, level_count - 1, axis=0))

    def before(v):
        return pltpu.roll(v, 1, axis=1)

    def after(v):
        return pltpu.roll(v, lanes - 1, axis=1)

    x_flux = [flux(face(inc[k], inc[k + 1]), face(cells[k], cells[k + 1]), 0) for k in range(3)]
    for x in range(2):
        own_inc, own = inc[x + 1], cells[x + 1]
        inc_before, own_before = [before(v) for v in own_inc], [before(v) for v in own]
        y_lower = flux(face(inc_before, own_inc), face(own_before, own), 1)
        inc_below, own_below = [below(v) for v in own_inc], [below(v) for v in own]
        inc_above, own_above = [above(v) for v in own_inc], [above(v) for v in own]
        z_lower = flux(face(inc_below, own_inc), face(own_below, own), 2)
        z_upper = flux(face(own_inc, inc_above), face(own, own_above), 2)
        for c in range(3):
            twice = 2.0 * own[c]
            tendency = -(x_flux[x + 1][c] - x_flux[x][c])
            tendency += viscosity * (cells[x][c] + cells[x + 2][c] - twice)
            tendency -= after(y_lower[c]) - y_lower[c]
            tendency += viscosity * (own_before[c] + after(own[c]) - twice)
            tendency -= (z_upper[c] - z_lower[c]) / cell_height
            tendency += viscosity * (own_below[c] + own_above[c] - twice) / cell_height**2
            result = own[c] + time_step * tendency
            incident[x, c] = own_inc[c][:, 1 : y_tile + 1]
            predicted[x, c] = result[:, 1 : y_tile + 1]


def swaps(size, first):
    pairs = [(i, i + 1) for i in range(first, size - 1, 2)]
    return pairs + [(j, i) for i, j in pairs]


PAIRS = (("ky", 0), ("ky", 1), ("gz", 0), ("gz", 1))
ORDER = (("gz", 1), ("gz", 0), ("ky", 1), ("ky", 0))


def on_device(amplitudes, complementary):
    x_tile, level_count, _, y_tile = complementary.shape
    ky_groups, gz_groups = lax.axis_size("ky"), lax.axis_size("gz")
    wave_local, kx_count = amplitudes.shape[1:]
    wave_count = wave_local * ky_groups
    height = -(-(y_tile + 2) // 16) * 16
    chunk = 4 * 2 * wave_local * 3 * level_count // lanes
    vmem = pl.BlockSpec(memory_space=pltpu.VMEM)
    anywhere = pl.BlockSpec(memory_space=pl.ANY)

    def x_call(*refs):
        x_kernel(ky_groups, level_count, wave_count, *refs)

    def y_call(*refs):
        y_kernel(ky_groups, wave_local, height, *refs)

    comp = jnp.transpose(complementary, (0, 2, 1, 3)).reshape(x_tile, 3 * level_count, y_tile)
    with jax.named_scope("x_transform"):
        sent = pl.pallas_call(
            x_call,
            out_shape=jax.ShapeDtypeStruct((ky_groups * chunk, lanes), f32),
            in_specs=[anywhere],
            out_specs=vmem,
            scratch_shapes=[
                pltpu.VMEM(amplitudes.shape, f32),
                pltpu.SemaphoreType.DMA,
            ],
            name="x_transform",
        )(amplitudes)
    halos = [
        lax.ppermute(comp, axis, swaps(lax.axis_size(axis), first)) for axis, first in ORDER
    ]
    x_in, x_out, y_in, y_out = (halos[ORDER.index(which)] for which in PAIRS)
    received = lax.all_to_all(sent.reshape(ky_groups, 1, chunk * lanes), "ky", 0, 0)
    result = jax.ShapeDtypeStruct((x_tile, 3, level_count, y_tile), f32)
    with jax.named_scope("y_transform_and_step"):
        incident, predicted = pl.pallas_call(
            y_call,
            out_shape=(result, result),
            in_specs=[vmem] * 6,
            out_specs=(vmem, vmem),
            scratch_shapes=[pltpu.VMEM((4, 3 * level_count, lanes), f32)],
            compiler_params=pltpu.CompilerParams(vmem_limit_bytes=48 * 2**20),
            name="y_transform",
        )(received.reshape(ky_groups * chunk, lanes), comp, y_out, y_in, x_out, x_in)
    back = (0, 2, 1, 3)
    return jnp.transpose(incident, back), jnp.transpose(predicted, back)


def solution(mesh):
    placed = (P(None, "ky", None), P("ky", None, None, "gz"))
    return jax.shard_map(
        on_device,
        mesh=mesh,
        in_specs=placed,
        out_specs=(P("ky", None, None, "gz"), P("ky", None, None, "gz")),
        check_vma=False,
    )
```

```python
import jax
import jax.numpy as jnp
import numpy as np
from jax import lax
from jax.experimental import pallas as pl
from jax.experimental.pallas import tpu as pltpu
from jax.sharding import PartitionSpec as P

band_factor = 16.0
cell_height = 0.125
time_step = 0.05
viscosity = 0.02
lanes = 128
f32 = jnp.float32


def split(x):
    high = x.astype(jnp.bfloat16)
    return high, (x - high.astype(f32)).astype(jnp.bfloat16)


def cos_sin(turns, period):
    quarter = period // 4
    turns = turns & (period - 1)
    which = ((turns + quarter // 2) // quarter) & 3
    angle = (turns - (turns + quarter // 2) // quarter * quarter).astype(f32) * (2.0 * np.pi / period)
    square = angle * angle
    sin, cos = jnp.full_like(square, 1.0), jnp.full_like(square, 1.0)
    for n in (8, 6, 4, 2):
        sin = 1.0 - sin * square * (1.0 / (n * (n + 1)))
    for n in (9, 7, 5, 3, 1):
        cos = 1.0 - cos * square * (1.0 / (n * (n + 1)))
    sin = sin * angle
    swapped = (which & 1) == 1
    first, second = jnp.where(swapped, sin, cos), jnp.where(swapped, cos, sin)
    return (
        jnp.where((which == 1) | (which == 2), -first, first),
        jnp.where(which >= 2, -second, second),
    )


def x_tables(ky_groups, kx_count, centre):
    period = int(2 * band_factor * kx_count)
    row = lax.broadcasted_iota(jnp.int32, (32, kx_count), 0)
    halves = jnp.where(row < 16, row % 8 * 4 + row // 8 * 2 + 1, 32 * (row - 16))
    halves = jnp.where(row < 24, halves, 2 * centre)
    cos, sin = cos_sin(halves * lax.broadcasted_iota(jnp.int32, (32, kx_count), 1), period)
    cos_rows, sin_rows = [], []
    for e in range(2):
        near = slice(8 * e, 8 * e + 8)
        for i in range(ky_groups // 16):
            far = slice(16 + i, 17 + i)
            cos_rows.append(cos[near] * cos[far] - sin[near] * sin[far])
            sin_rows.append(sin[near] * cos[far] + cos[near] * sin[far])
    return jnp.concatenate(cos_rows + sin_rows, axis=0), cos[24:], sin[24:]


def y_tables(y_tile, ky_groups, wave_local, height):
    wave_count = ky_groups * wave_local
    shape = (height, wave_count)
    row, column = (lax.broadcasted_iota(jnp.int32, shape, axis) for axis in (0, 1))
    cell = lax.axis_index("gz") * y_tile + row - 1
    inside = (cell >= 0) & (cell < lax.axis_size("gz") * y_tile) & (row < y_tile + 2)
    source = column % ky_groups
    source = jnp.where(source < ky_groups // 2, ky_groups // 2 - 1 - source, source)
    wave = source * wave_local + column // ky_groups - wave_count // 2
    cos, sin = cos_sin((2 * cell + 1) * wave, int(2 * band_factor * wave_count))
    return jnp.concatenate([jnp.where(inside, cos, 0.0), jnp.where(inside, -sin, 0.0)], axis=1)


def dot_nt(a, b):
    return lax.dot_general(a, b, (((1,), (1,)), ((), ())), preferred_element_type=f32)


def x_kernel(ky_groups, level_count, wave_count, amplitudes, out, modes, sem):
    copy = pltpu.make_async_copy(amplitudes, modes, sem)
    copy.start()
    wave_local, kx_count = amplitudes.shape[1:]
    per_row = 3 * level_count
    me = lax.axis_index("ky")
    rows = (me * wave_local + lax.broadcasted_iota(jnp.int32, (wave_local, kx_count), 0)).astype(f32)
    step_y = 2.0 * np.pi / (band_factor * wave_count)
    step_x = 2.0 * np.pi / (band_factor * kx_count)
    along_y = (rows - wave_count / 2.0) * step_y
    columns = lax.broadcasted_iota(jnp.int32, (wave_local, kx_count), 1).astype(f32)
    along_x = columns * step_x
    magnitude = jnp.sqrt(along_x * along_x + along_y * along_y)
    shape = (level_count, kx_count)
    depths = -(lax.broadcasted_iota(jnp.int32, shape, 0).astype(f32) + 0.5) * cell_height
    kx = along_x[0:1]
    decays = [jnp.exp(jnp.broadcast_to(magnitude[n : n + 1], shape) * depths) for n in range(wave_local)]
    table, cos_centre, sin_centre = x_tables(ky_groups, kx_count, ky_groups)
    table_hi, table_lo = split(table)
    copy.wait()
    all_re = modes[0] * cos_centre - modes[1] * sin_centre
    all_im = modes[0] * sin_centre + modes[1] * cos_centre
    parts_re, parts_im = [], []
    for n in range(wave_local):
        k = magnitude[n : n + 1]
        ky = along_y[n : n + 1]
        re = decays[n] * all_re[n : n + 1]
        im = decays[n] * all_im[n : n + 1]
        parts_re += [-kx * im, -ky * im, k * re]
        parts_im += [kx * re, ky * re, k * im]
    modes_hi, modes_lo = split(jnp.concatenate(parts_re + parts_im, axis=0))
    product = dot_nt(table_hi, modes_hi)
    product += dot_nt(table_hi, modes_lo) + dot_nt(table_lo, modes_hi)
    half = product.shape[0] // 2
    by_cos, by_sin = product[:half], product[half:]
    middle = wave_local * per_row
    turned = jnp.concatenate([-by_sin[:, middle:], by_sin[:, :middle]], axis=1)
    upper, lower = by_cos + turned, by_cos - turned
    count = ky_groups // 2
    upper_first, upper_second = upper[:count], upper[count:]
    lower_second, lower_first = lower[:count], lower[count:]
    width = upper.shape[1] // lanes
    chunk = 4 * width
    for j in range(width):
        cut = slice(lanes * j, lanes * (j + 1))
        out[pl.ds(j, count - 1, stride=chunk), :] = lower_second[1:, cut]
        out[pl.ds(j + (count - 1) * chunk, 1), :] = jnp.zeros((1, lanes), f32)
        out[pl.ds(j + width, count, stride=chunk), :] = lower_first[:, cut]
        out[pl.ds(j + 2 * width, count, stride=chunk), :] = lower_second[:, cut]
        out[pl.ds(j + 3 * width, 1), :] = upper_first[:1, cut]
        out[pl.ds(j + chunk + 3 * width, count - 1, stride=chunk), :] = lower_first[: count - 1, cut]
        at = count * chunk + j
        out[pl.ds(at, 1), :] = lower_second[:1, cut]
        out[pl.ds(at + chunk, count - 1, stride=chunk), :] = upper_second[: count - 1, cut]
        out[pl.ds(at + width, count, stride=chunk), :] = upper_first[:, cut]
        out[pl.ds(at + 2 * width, count, stride=chunk), :] = upper_second[:, cut]
        out[pl.ds(at + 3 * width, count - 1, stride=chunk), :] = upper_first[1:, cut]
        out[pl.ds(at + (count - 1) * chunk + 3 * width, 1), :] = jnp.zeros((1, lanes), f32)


def face(a, b):
    return [0.5 * (p + q) for p, q in zip(a, b)]


def flux(inc, comp, normal):
    total = inc[normal] + comp[normal]
    return [total * comp[c] + comp[normal] * inc[c] for c in range(3)]


def y_kernel(ky_groups, wave_local, height, received, comp, y_out, y_in, x_out, x_in, incident, predicted, padded):
    per_row, y_tile = comp.shape[1:]
    level_count = per_row // 3
    width = 2 * wave_local * per_row // lanes
    chunk = 4 * width
    cols = [[received[pl.ds(k * width + t, ky_groups, stride=chunk), :] for t in range(width)] for k in range(4)]
    lane = lax.broadcasted_iota(jnp.int32, (ky_groups, lanes), 1)
    blocks = []
    for b in range(2 * wave_local):
        first, offset = divmod(b * per_row, lanes)
        block = None
        for k in range(4):
            at = k * per_row
            shift = (at - offset) % lanes
            piece = pltpu.roll(cols[k][first], shift, axis=1) if shift else cols[k][first]
            if offset + per_row > lanes:
                rest = pltpu.roll(cols[k][first + 1], shift, axis=1) if shift else cols[k][first + 1]
                piece = jnp.where(lane < at + lanes - offset, piece, rest)
            block = piece if block is None else jnp.where(lane < at, block, piece)
        blocks.append(block)
    modes_hi, modes_lo = split(jnp.concatenate(blocks, axis=0))
    table_hi, table_lo = split(y_tables(y_tile, ky_groups, wave_local, height))
    both = jnp.dot(jnp.concatenate([table_hi, table_lo], axis=0), modes_hi, preferred_element_type=f32)
    field = both[:height] + both[height:]
    field += jnp.dot(table_hi, modes_lo, preferred_element_type=f32)
    field = jnp.concatenate([field, jnp.zeros((lanes - height, lanes), f32)], axis=0).T
    inc = [
        [field[(k * 3 + c) * level_count : (k * 3 + c + 1) * level_count] for c in range(3)]
        for k in range(4)
    ]
    padded[...] = jnp.zeros_like(padded)
    x_even = lax.axis_index("ky") % 2 == 0
    y_even = lax.axis_index("gz") % 2 == 0
    inner = slice(1, y_tile + 1)
    padded[0, :, inner] = jnp.where(x_even, x_out[1], x_in[1])
    padded[3, :, inner] = jnp.where(x_even, x_in[0], x_out[0])
    for x in range(2):
        padded[x + 1, :, inner] = comp[x]
        padded[x + 1, :, 0:1] = jnp.where(y_even, y_out[x], y_in[x])[:, y_tile - 1 : y_tile]
        padded[x + 1, :, y_tile + 1 : y_tile + 2] = jnp.where(y_even, y_in[x], y_out[x])[:, 0:1]
    cells = [[padded[k, c * level_count : (c + 1) * level_count] for c in range(3)] for k in range(4)]
    level = lax.broadcasted_iota(jnp.int32, (level_count, lanes), 0)

    def below(v):
        return jnp.where(level == 0, 0.0, pltpu.roll(v, 1, axis=0))

    def above(v):
        return jnp.where(level == level_count - 1, 0.0, pltpu.roll(v, level_count - 1, axis=0))

    def before(v):
        return pltpu.roll(v, 1, axis=1)

    def after(v):
        return pltpu.roll(v, lanes - 1, axis=1)

    x_flux = [flux(face(inc[k], inc[k + 1]), face(cells[k], cells[k + 1]), 0) for k in range(3)]
    for x in range(2):
        own_inc, own = inc[x + 1], cells[x + 1]
        inc_before, own_before = [before(v) for v in own_inc], [before(v) for v in own]
        y_lower = flux(face(inc_before, own_inc), face(own_before, own), 1)
        inc_below, own_below = [below(v) for v in own_inc], [below(v) for v in own]
        inc_above, own_above = [above(v) for v in own_inc], [above(v) for v in own]
        z_lower = flux(face(inc_below, own_inc), face(own_below, own), 2)
        z_upper = flux(face(own_inc, inc_above), face(own, own_above), 2)
        for c in range(3):
            twice = 2.0 * own[c]
            tendency = -(x_flux[x + 1][c] - x_flux[x][c])
            tendency += viscosity * (cells[x][c] + cells[x + 2][c] - twice)
            tendency -= after(y_lower[c]) - y_lower[c]
            tendency += viscosity * (own_before[c] + after(own[c]) - twice)
            tendency -= (z_upper[c] - z_lower[c]) / cell_height
            tendency += viscosity * (own_below[c] + own_above[c] - twice) / cell_height**2
            result = own[c] + time_step * tendency
            incident[x, c] = own_inc[c][:, 1 : y_tile + 1]
            predicted[x, c] = result[:, 1 : y_tile + 1]


def swaps(size, first):
    pairs = [(i, i + 1) for i in range(first, size - 1, 2)]
    return pairs + [(j, i) for i, j in pairs]


PAIRS = (("ky", 0), ("ky", 1), ("gz", 0), ("gz", 1))
ORDER = (("gz", 1), ("gz", 0), ("ky", 1), ("ky", 0))


def on_device(amplitudes, complementary):
    x_tile, level_count, _, y_tile = complementary.shape
    ky_groups, gz_groups = lax.axis_size("ky"), lax.axis_size("gz")
    wave_local, kx_count = amplitudes.shape[1:]
    wave_count = wave_local * ky_groups
    height = -(-(y_tile + 2) // 16) * 16
    chunk = 4 * 2 * wave_local * 3 * level_count // lanes
    vmem = pl.BlockSpec(memory_space=pltpu.VMEM)
    anywhere = pl.BlockSpec(memory_space=pl.ANY)

    def x_call(*refs):
        x_kernel(ky_groups, level_count, wave_count, *refs)

    def y_call(*refs):
        y_kernel(ky_groups, wave_local, height, *refs)

    comp = jnp.transpose(complementary, (0, 2, 1, 3)).reshape(x_tile, 3 * level_count, y_tile)
    with jax.named_scope("x_transform"):
        sent = pl.pallas_call(
            x_call,
            out_shape=jax.ShapeDtypeStruct((ky_groups * chunk, lanes), f32),
            in_specs=[anywhere],
            out_specs=vmem,
            scratch_shapes=[
                pltpu.VMEM(amplitudes.shape, f32),
                pltpu.SemaphoreType.DMA,
            ],
            name="x_transform",
        )(amplitudes)
    halos = [
        lax.ppermute(comp, axis, swaps(lax.axis_size(axis), first)) for axis, first in ORDER
    ]
    x_in, x_out, y_in, y_out = (halos[ORDER.index(which)] for which in PAIRS)
    order = [*range(ky_groups // 2 - 1, -1, -1), *range(ky_groups // 2, ky_groups)]
    sent = sent.reshape(ky_groups, 1, chunk * lanes)
    received = lax.all_to_all(sent, "ky", 0, 0, axis_index_groups=[order])
    result = jax.ShapeDtypeStruct((x_tile, 3, level_count, y_tile), f32)
    with jax.named_scope("y_transform_and_step"):
        incident, predicted = pl.pallas_call(
            y_call,
            out_shape=(result, result),
            in_specs=[vmem] * 6,
            out_specs=(vmem, vmem),
            scratch_shapes=[pltpu.VMEM((4, 3 * level_count, lanes), f32)],
            compiler_params=pltpu.CompilerParams(vmem_limit_bytes=48 * 2**20),
            name="y_transform",
        )(received.reshape(ky_groups * chunk, lanes), comp, y_out, y_in, x_out, x_in)
    back = (0, 2, 1, 3)
    return jnp.transpose(incident, back), jnp.transpose(predicted, back)


def solution(mesh):
    placed = (P(None, "ky", None), P("ky", None, None, "gz"))
    return jax.shard_map(
        on_device,
        mesh=mesh,
        in_specs=placed,
        out_specs=(P("ky", None, None, "gz"), P("ky", None, None, "gz")),
        check_vma=False,
    )
```

```python
import jax
import jax.numpy as jnp
import numpy as np
from jax import lax
from jax.experimental import pallas as pl
from jax.experimental.pallas import tpu as pltpu
from jax.sharding import PartitionSpec as P

band_factor = 16.0
cell_height = 0.125
time_step = 0.05
viscosity = 0.02
lanes = 128
f32 = jnp.float32


def split(x):
    high = x.astype(jnp.bfloat16)
    return high, (x - high.astype(f32)).astype(jnp.bfloat16)


def cos_sin(turns, period):
    quarter = period // 4
    turns = turns & (period - 1)
    which = ((turns + quarter // 2) // quarter) & 3
    angle = (turns - (turns + quarter // 2) // quarter * quarter).astype(f32) * (2.0 * np.pi / period)
    square = angle * angle
    sin, cos = jnp.full_like(square, 1.0), jnp.full_like(square, 1.0)
    for n in (8, 6, 4, 2):
        sin = 1.0 - sin * square * (1.0 / (n * (n + 1)))
    for n in (9, 7, 5, 3, 1):
        cos = 1.0 - cos * square * (1.0 / (n * (n + 1)))
    sin = sin * angle
    swapped = (which & 1) == 1
    first, second = jnp.where(swapped, sin, cos), jnp.where(swapped, cos, sin)
    return (
        jnp.where((which == 1) | (which == 2), -first, first),
        jnp.where(which >= 2, -second, second),
    )


def x_tables(ky_groups, kx_count, centre):
    period = int(2 * band_factor * kx_count)
    row = lax.broadcasted_iota(jnp.int32, (32, kx_count), 0)
    halves = jnp.where(row < 16, row % 8 * 4 + row // 8 * 2 + 1, 32 * (row - 16))
    halves = jnp.where(row < 24, halves, 2 * centre)
    cos, sin = cos_sin(halves * lax.broadcasted_iota(jnp.int32, (32, kx_count), 1), period)
    cos_rows, sin_rows = [], []
    for e in range(2):
        near = slice(8 * e, 8 * e + 8)
        for i in range(ky_groups // 16):
            far = slice(16 + i, 17 + i)
            cos_rows.append(cos[near] * cos[far] - sin[near] * sin[far])
            sin_rows.append(sin[near] * cos[far] + cos[near] * sin[far])
    return jnp.concatenate(cos_rows + sin_rows, axis=0), cos[24:], sin[24:]


def y_tables(y_tile, ky_groups, wave_local, height):
    wave_count = ky_groups * wave_local
    shape = (height, wave_count)
    row, column = (lax.broadcasted_iota(jnp.int32, shape, axis) for axis in (0, 1))
    cell = lax.axis_index("gz") * y_tile + row - 1
    inside = (cell >= 0) & (cell < lax.axis_size("gz") * y_tile) & (row < y_tile + 2)
    source = column % ky_groups
    source = jnp.where(source < ky_groups // 2, ky_groups // 2 - 1 - source, source)
    half = wave_count // 2
    row_local = column % half // ky_groups * 2 + column // half
    wave = source * wave_local + row_local - half
    cos, sin = cos_sin((2 * cell + 1) * wave, int(2 * band_factor * wave_count))
    cos, sin = jnp.where(inside, cos, 0.0), jnp.where(inside, -sin, 0.0)
    return [jnp.concatenate([cos[:, at : at + half], sin[:, at : at + half]], axis=1) for at in (0, half)]


def dot_nt(a, b):
    return lax.dot_general(a, b, (((1,), (1,)), ((), ())), preferred_element_type=f32)


def x_kernel(ky_groups, level_count, wave_count, amplitudes, out, modes, sem):
    wave_local, kx_count = amplitudes.shape[1:]
    copies = []
    for part in range(2):
        for column in range(0, kx_count, kx_count // 2):
            which = (part, slice(None), pl.ds(column, kx_count // 2))
            copies.append(pltpu.make_async_copy(amplitudes.at[which], modes.at[which], sem.at[len(copies)]))
            copies[-1].start()
    per_row = 3 * level_count
    me = lax.axis_index("ky")
    rows = (me * wave_local + lax.broadcasted_iota(jnp.int32, (wave_local, kx_count), 0)).astype(f32)
    step_y = 2.0 * np.pi / (band_factor * wave_count)
    step_x = 2.0 * np.pi / (band_factor * kx_count)
    along_y = (rows - wave_count / 2.0) * step_y
    columns = lax.broadcasted_iota(jnp.int32, (wave_local, kx_count), 1).astype(f32)
    along_x = columns * step_x
    magnitude = jnp.sqrt(along_x * along_x + along_y * along_y)
    shape = (level_count, kx_count)
    depths = -(lax.broadcasted_iota(jnp.int32, shape, 0).astype(f32) + 0.5) * cell_height
    kx = along_x[0:1]
    decays = [jnp.exp(jnp.broadcast_to(magnitude[n : n + 1], shape) * depths) for n in range(wave_local)]
    table, cos_centre, sin_centre = x_tables(ky_groups, kx_count, ky_groups)
    table_hi, table_lo = split(table)
    for copy in copies:
        copy.wait()
    all_re = modes[0] * cos_centre - modes[1] * sin_centre
    all_im = modes[0] * sin_centre + modes[1] * cos_centre
    parts_re, parts_im = [], []
    for n in range(wave_local):
        k = magnitude[n : n + 1]
        ky = along_y[n : n + 1]
        re = decays[n] * all_re[n : n + 1]
        im = decays[n] * all_im[n : n + 1]
        parts_re += [-kx * im, -ky * im, k * re]
        parts_im += [kx * re, ky * re, k * im]
    modes_hi, modes_lo = split(jnp.concatenate(parts_re + parts_im, axis=0))
    product = dot_nt(table_hi, modes_hi)
    product += dot_nt(table_hi, modes_lo) + dot_nt(table_lo, modes_hi)
    half = product.shape[0] // 2
    by_cos, by_sin = product[:half], product[half:]
    middle = wave_local * per_row
    turned = jnp.concatenate([-by_sin[:, middle:], by_sin[:, :middle]], axis=1)
    upper, lower = by_cos + turned, by_cos - turned
    count = ky_groups // 2
    upper_first, upper_second = upper[:count], upper[count:]
    lower_second, lower_first = lower[:count], lower[count:]
    width = upper.shape[1] // lanes
    chunk = 4 * width
    for j in range(width):
        cut = slice(lanes * j, lanes * (j + 1))
        out[pl.ds(j, count - 1, stride=chunk), :] = lower_second[1:, cut]
        out[pl.ds(j + (count - 1) * chunk, 1), :] = jnp.zeros((1, lanes), f32)
        out[pl.ds(j + width, count, stride=chunk), :] = lower_first[:, cut]
        out[pl.ds(j + 2 * width, count, stride=chunk), :] = lower_second[:, cut]
        out[pl.ds(j + 3 * width, 1), :] = upper_first[:1, cut]
        out[pl.ds(j + chunk + 3 * width, count - 1, stride=chunk), :] = lower_first[: count - 1, cut]
        at = count * chunk + j
        out[pl.ds(at, 1), :] = lower_second[:1, cut]
        out[pl.ds(at + chunk, count - 1, stride=chunk), :] = upper_second[: count - 1, cut]
        out[pl.ds(at + width, count, stride=chunk), :] = upper_first[:, cut]
        out[pl.ds(at + 2 * width, count, stride=chunk), :] = upper_second[:, cut]
        out[pl.ds(at + 3 * width, count - 1, stride=chunk), :] = upper_first[1:, cut]
        out[pl.ds(at + (count - 1) * chunk + 3 * width, 1), :] = jnp.zeros((1, lanes), f32)


def face(a, b):
    return [0.5 * (p + q) for p, q in zip(a, b)]


def flux(inc, comp, normal):
    total = inc[normal] + comp[normal]
    return [total * comp[c] + comp[normal] * inc[c] for c in range(3)]


def y_kernel(ky_groups, wave_local, height, received, comp, y_out, y_in, x_out, x_in, incident, predicted, padded):
    per_row, y_tile = comp.shape[1:]
    level_count = per_row // 3
    width = 2 * wave_local * per_row // lanes
    chunk = 4 * width
    cols = [[received[pl.ds(k * width + t, ky_groups, stride=chunk), :] for t in range(width)] for k in range(4)]
    lane = lax.broadcasted_iota(jnp.int32, (ky_groups, lanes), 1)
    blocks = []
    pair = 2 * per_row
    for b in range(wave_local):
        first, offset = divmod(b * pair, lanes)
        sides = []
        for k in range(4):
            at = k % 2 * pair
            shift = (at - offset) % lanes
            piece = pltpu.roll(cols[k][first], shift, axis=1) if shift else cols[k][first]
            if offset + pair > lanes:
                rest = pltpu.roll(cols[k][first + 1], shift, axis=1) if shift else cols[k][first + 1]
                piece = jnp.where(lane < at + lanes - offset, piece, rest)
            sides.append(piece if k % 2 == 0 else jnp.where(lane < at, sides.pop(), piece))
        blocks.append(jnp.concatenate(sides, axis=1))
    modes_hi, modes_lo = split(jnp.concatenate(blocks, axis=0))
    tables = y_tables(y_tile, ky_groups, wave_local, height)
    table_hi, table_lo = split(jnp.concatenate(tables, axis=0))
    both = jnp.dot(jnp.concatenate([table_hi, table_lo], axis=0), modes_hi, preferred_element_type=f32)
    field = both[: 2 * height] + both[2 * height :]
    field += jnp.dot(table_hi, modes_lo, preferred_element_type=f32)
    even, odd = field[:height], field[height:]
    sides = [slice(side, side + lanes) for side in (0, lanes)]
    field = [even[:, side] + pltpu.roll(odd[:, side], lanes - per_row, axis=1) for side in sides]
    below_it = jnp.zeros((lanes - height, lanes), f32)
    field = [jnp.concatenate([side, below_it], axis=0).T for side in field]
    starts = [(k // 2, k % 2 * pair) for k in range(4)]
    inc = [
        [field[side][at + c * level_count : at + (c + 1) * level_count] for c in range(3)]
        for side, at in starts
    ]
    padded[...] = jnp.zeros_like(padded)
    x_even = lax.axis_index("ky") % 2 == 0
    y_even = lax.axis_index("gz") % 2 == 0
    inner = slice(1, y_tile + 1)
    padded[0, :, inner] = jnp.where(x_even, x_out[1], x_in[1])
    padded[3, :, inner] = jnp.where(x_even, x_in[0], x_out[0])
    for x in range(2):
        padded[x + 1, :, inner] = comp[x]
        padded[x + 1, :, 0:1] = jnp.where(y_even, y_out[x], y_in[x])[:, y_tile - 1 : y_tile]
        padded[x + 1, :, y_tile + 1 : y_tile + 2] = jnp.where(y_even, y_in[x], y_out[x])[:, 0:1]
    cells = [[padded[k, c * level_count : (c + 1) * level_count] for c in range(3)] for k in range(4)]
    level = lax.broadcasted_iota(jnp.int32, (level_count, lanes), 0)

    def below(v):
        return jnp.where(level == 0, 0.0, pltpu.roll(v, 1, axis=0))

    def above(v):
        return jnp.where(level == level_count - 1, 0.0, pltpu.roll(v, level_count - 1, axis=0))

    def before(v):
        return pltpu.roll(v, 1, axis=1)

    def after(v):
        return pltpu.roll(v, lanes - 1, axis=1)

    x_flux = [flux(face(inc[k], inc[k + 1]), face(cells[k], cells[k + 1]), 0) for k in range(3)]
    for x in range(2):
        own_inc, own = inc[x + 1], cells[x + 1]
        inc_before, own_before = [before(v) for v in own_inc], [before(v) for v in own]
        y_lower = flux(face(inc_before, own_inc), face(own_before, own), 1)
        inc_below, own_below = [below(v) for v in own_inc], [below(v) for v in own]
        inc_above, own_above = [above(v) for v in own_inc], [above(v) for v in own]
        z_lower = flux(face(inc_below, own_inc), face(own_below, own), 2)
        z_upper = flux(face(own_inc, inc_above), face(own, own_above), 2)
        for c in range(3):
            twice = 2.0 * own[c]
            tendency = -(x_flux[x + 1][c] - x_flux[x][c])
            tendency += viscosity * (cells[x][c] + cells[x + 2][c] - twice)
            tendency -= after(y_lower[c]) - y_lower[c]
            tendency += viscosity * (own_before[c] + after(own[c]) - twice)
            tendency -= (z_upper[c] - z_lower[c]) / cell_height
            tendency += viscosity * (own_below[c] + own_above[c] - twice) / cell_height**2
            result = own[c] + time_step * tendency
            incident[x, c] = own_inc[c][:, 1 : y_tile + 1]
            predicted[x, c] = result[:, 1 : y_tile + 1]


def swaps(size, first):
    pairs = [(i, i + 1) for i in range(first, size - 1, 2)]
    return pairs + [(j, i) for i, j in pairs]


PAIRS = (("ky", 0), ("ky", 1), ("gz", 0), ("gz", 1))
ORDER = (("gz", 1), ("gz", 0), ("ky", 1), ("ky", 0))


def on_device(amplitudes, complementary):
    x_tile, level_count, _, y_tile = complementary.shape
    ky_groups, gz_groups = lax.axis_size("ky"), lax.axis_size("gz")
    wave_local, kx_count = amplitudes.shape[1:]
    wave_count = wave_local * ky_groups
    height = -(-(y_tile + 2) // 16) * 16
    chunk = 4 * 2 * wave_local * 3 * level_count // lanes
    vmem = pl.BlockSpec(memory_space=pltpu.VMEM)
    anywhere = pl.BlockSpec(memory_space=pl.ANY)

    def x_call(*refs):
        x_kernel(ky_groups, level_count, wave_count, *refs)

    def y_call(*refs):
        y_kernel(ky_groups, wave_local, height, *refs)

    comp = jnp.transpose(complementary, (0, 2, 1, 3)).reshape(x_tile, 3 * level_count, y_tile)
    with jax.named_scope("x_transform"):
        sent = pl.pallas_call(
            x_call,
            out_shape=jax.ShapeDtypeStruct((ky_groups * chunk, lanes), f32),
            in_specs=[anywhere],
            out_specs=vmem,
            scratch_shapes=[
                pltpu.VMEM(amplitudes.shape, f32),
                pltpu.SemaphoreType.DMA((4,)),
            ],
            name="x_transform",
        )(amplitudes)
    halos = [
        lax.ppermute(comp, axis, swaps(lax.axis_size(axis), first)) for axis, first in ORDER
    ]
    x_in, x_out, y_in, y_out = (halos[ORDER.index(which)] for which in PAIRS)
    order = [*range(ky_groups // 2 - 1, -1, -1), *range(ky_groups // 2, ky_groups)]
    sent = sent.reshape(ky_groups, 1, chunk * lanes)
    received = lax.all_to_all(sent, "ky", 0, 0, axis_index_groups=[order])
    result = jax.ShapeDtypeStruct((x_tile, 3, level_count, y_tile), f32)
    with jax.named_scope("y_transform_and_step"):
        incident, predicted = pl.pallas_call(
            y_call,
            out_shape=(result, result),
            in_specs=[vmem] * 6,
            out_specs=(vmem, vmem),
            scratch_shapes=[pltpu.VMEM((4, 3 * level_count, lanes), f32)],
            compiler_params=pltpu.CompilerParams(vmem_limit_bytes=48 * 2**20),
            name="y_transform",
        )(received.reshape(ky_groups * chunk, lanes), comp, y_out, y_in, x_out, x_in)
    back = (0, 2, 1, 3)
    return jnp.transpose(incident, back), jnp.transpose(predicted, back)


def solution(mesh):
    placed = (P(None, "ky", None), P("ky", None, None, "gz"))
    return jax.shard_map(
        on_device,
        mesh=mesh,
        in_specs=placed,
        out_specs=(P("ky", None, None, "gz"), P("ky", None, None, "gz")),
        check_vma=False,
    )
```

```python
import jax
import jax.numpy as jnp
import numpy as np
from jax import lax
from jax.experimental import pallas as pl
from jax.experimental.pallas import tpu as pltpu
from jax.sharding import PartitionSpec as P

band_factor = 16.0
cell_height = 0.125
time_step = 0.05
viscosity = 0.02
lanes = 128
f32 = jnp.float32


def split(x):
    high = x.astype(jnp.bfloat16)
    return high, (x - high.astype(f32)).astype(jnp.bfloat16)


def cos_sin(turns, period):
    quarter = period // 4
    turns = turns & (period - 1)
    which = ((turns + quarter // 2) // quarter) & 3
    angle = (turns - (turns + quarter // 2) // quarter * quarter).astype(f32) * (2.0 * np.pi / period)
    square = angle * angle
    sin, cos = jnp.full_like(square, 1.0), jnp.full_like(square, 1.0)
    for n in (8, 6, 4, 2):
        sin = 1.0 - sin * square * (1.0 / (n * (n + 1)))
    for n in (9, 7, 5, 3, 1):
        cos = 1.0 - cos * square * (1.0 / (n * (n + 1)))
    sin = sin * angle
    swapped = (which & 1) == 1
    first, second = jnp.where(swapped, sin, cos), jnp.where(swapped, cos, sin)
    return (
        jnp.where((which == 1) | (which == 2), -first, first),
        jnp.where(which >= 2, -second, second),
    )


def x_tables(ky_groups, kx_count, centre):
    period = int(2 * band_factor * kx_count)
    row = lax.broadcasted_iota(jnp.int32, (32, kx_count), 0)
    halves = jnp.where(row < 16, row % 8 * 4 + row // 8 * 2 + 1, 32 * (row - 16))
    halves = jnp.where(row < 24, halves, 2 * centre)
    cos, sin = cos_sin(halves * lax.broadcasted_iota(jnp.int32, (32, kx_count), 1), period)
    cos_rows, sin_rows = [], []
    for e in range(2):
        near = slice(8 * e, 8 * e + 8)
        for i in range(ky_groups // 16):
            far = slice(16 + i, 17 + i)
            cos_rows.append(cos[near] * cos[far] - sin[near] * sin[far])
            sin_rows.append(sin[near] * cos[far] + cos[near] * sin[far])
    return jnp.concatenate(cos_rows + sin_rows, axis=0), cos[24:], sin[24:]


def y_tables(y_tile, ky_groups, wave_local, height):
    wave_count = ky_groups * wave_local
    shape = (height, wave_count)
    row, column = (lax.broadcasted_iota(jnp.int32, shape, axis) for axis in (0, 1))
    cell = lax.axis_index("gz") * y_tile + row - 1
    inside = (cell >= 0) & (cell < lax.axis_size("gz") * y_tile) & (row < y_tile + 2)
    source = column % ky_groups
    source = jnp.where(source < ky_groups // 2, ky_groups // 2 - 1 - source, source)
    half = wave_count // 2
    row_local = column % half // ky_groups * 2 + column // half
    wave = source * wave_local + row_local - half
    cos, sin = cos_sin((2 * cell + 1) * wave, int(2 * band_factor * wave_count))
    cos, sin = jnp.where(inside, cos, 0.0), jnp.where(inside, -sin, 0.0)
    return [jnp.concatenate([cos[:, at : at + half], sin[:, at : at + half]], axis=1) for at in (0, half)]


def dot_nt(a, b):
    return lax.dot_general(a, b, (((1,), (1,)), ((), ())), preferred_element_type=f32)


def x_kernel(ky_groups, level_count, wave_count, amplitudes, out, modes, sem):
    wave_local, kx_count = amplitudes.shape[1:]
    copies = []
    for part in range(2):
        for column in range(0, kx_count, kx_count // 2):
            which = (part, slice(None), pl.ds(column, kx_count // 2))
            copies.append(pltpu.make_async_copy(amplitudes.at[which], modes.at[which], sem.at[len(copies)]))
            copies[-1].start()
    per_row = 3 * level_count
    me = lax.axis_index("ky")
    rows = (me * wave_local + lax.broadcasted_iota(jnp.int32, (wave_local, kx_count), 0)).astype(f32)
    step_y = 2.0 * np.pi / (band_factor * wave_count)
    step_x = 2.0 * np.pi / (band_factor * kx_count)
    along_y = (rows - wave_count / 2.0) * step_y
    columns = lax.broadcasted_iota(jnp.int32, (wave_local, kx_count), 1).astype(f32)
    along_x = columns * step_x
    magnitude = jnp.sqrt(along_x * along_x + along_y * along_y)
    shape = (level_count, kx_count)
    depths = -(lax.broadcasted_iota(jnp.int32, shape, 0).astype(f32) + 0.5) * cell_height
    kx = along_x[0:1]
    decays = [jnp.exp(jnp.broadcast_to(magnitude[n : n + 1], shape) * depths) for n in range(wave_local)]
    table, cos_centre, sin_centre = x_tables(ky_groups, kx_count, ky_groups)
    table_hi, table_lo = split(table)
    for copy in copies:
        copy.wait()
    all_re = modes[0] * cos_centre - modes[1] * sin_centre
    all_im = modes[0] * sin_centre + modes[1] * cos_centre
    parts_re, parts_im = [], []
    for n in range(wave_local):
        k = magnitude[n : n + 1]
        ky = along_y[n : n + 1]
        re = decays[n] * all_re[n : n + 1]
        im = decays[n] * all_im[n : n + 1]
        parts_re += [-kx * im, -ky * im, k * re]
        parts_im += [kx * re, ky * re, k * im]
    modes_hi, modes_lo = split(jnp.concatenate(parts_re + parts_im, axis=0))
    both = dot_nt(jnp.concatenate([table_hi, table_lo], axis=0), modes_hi)
    product = both[: 2 * ky_groups] + both[2 * ky_groups :]
    product += dot_nt(table_hi, modes_lo)
    half = product.shape[0] // 2
    by_cos, by_sin = product[:half], product[half:]
    middle = wave_local * per_row
    turned = jnp.concatenate([-by_sin[:, middle:], by_sin[:, :middle]], axis=1)
    upper, lower = by_cos + turned, by_cos - turned
    count = ky_groups // 2
    upper_first, upper_second = upper[:count], upper[count:]
    lower_second, lower_first = lower[:count], lower[count:]
    width = upper.shape[1] // lanes
    chunk = 4 * width
    for j in range(width):
        cut = slice(lanes * j, lanes * (j + 1))
        out[pl.ds(j, count - 1, stride=chunk), :] = lower_second[1:, cut]
        out[pl.ds(j + (count - 1) * chunk, 1), :] = jnp.zeros((1, lanes), f32)
        out[pl.ds(j + width, count, stride=chunk), :] = lower_first[:, cut]
        out[pl.ds(j + 2 * width, count, stride=chunk), :] = lower_second[:, cut]
        out[pl.ds(j + 3 * width, 1), :] = upper_first[:1, cut]
        out[pl.ds(j + chunk + 3 * width, count - 1, stride=chunk), :] = lower_first[: count - 1, cut]
        at = count * chunk + j
        out[pl.ds(at, 1), :] = lower_second[:1, cut]
        out[pl.ds(at + chunk, count - 1, stride=chunk), :] = upper_second[: count - 1, cut]
        out[pl.ds(at + width, count, stride=chunk), :] = upper_first[:, cut]
        out[pl.ds(at + 2 * width, count, stride=chunk), :] = upper_second[:, cut]
        out[pl.ds(at + 3 * width, count - 1, stride=chunk), :] = upper_first[1:, cut]
        out[pl.ds(at + (count - 1) * chunk + 3 * width, 1), :] = jnp.zeros((1, lanes), f32)


def face(a, b):
    return [0.5 * (p + q) for p, q in zip(a, b)]


def flux(inc, comp, normal):
    total = inc[normal] + comp[normal]
    return [total * comp[c] + comp[normal] * inc[c] for c in range(3)]


def y_kernel(ky_groups, wave_local, height, received, comp, y_out, y_in, x_out, x_in, incident, predicted, padded):
    per_row, y_tile = comp.shape[1:]
    level_count = per_row // 3
    width = 2 * wave_local * per_row // lanes
    chunk = 4 * width
    cols = [[received[pl.ds(k * width + t, ky_groups, stride=chunk), :] for t in range(width)] for k in range(4)]
    lane = lax.broadcasted_iota(jnp.int32, (ky_groups, lanes), 1)
    blocks = []
    pair = 2 * per_row
    for b in range(wave_local):
        first, offset = divmod(b * pair, lanes)
        sides = []
        for k in range(4):
            at = k % 2 * pair
            shift = (at - offset) % lanes
            piece = pltpu.roll(cols[k][first], shift, axis=1) if shift else cols[k][first]
            if offset + pair > lanes:
                rest = pltpu.roll(cols[k][first + 1], shift, axis=1) if shift else cols[k][first + 1]
                piece = jnp.where(lane < at + lanes - offset, piece, rest)
            sides.append(piece if k % 2 == 0 else jnp.where(lane < at, sides.pop(), piece))
        blocks.append(jnp.concatenate(sides, axis=1))
    modes_hi, modes_lo = split(jnp.concatenate(blocks, axis=0))
    tables = y_tables(y_tile, ky_groups, wave_local, height)
    table_hi, table_lo = split(jnp.concatenate(tables, axis=0))
    both = jnp.dot(jnp.concatenate([table_hi, table_lo], axis=0), modes_hi, preferred_element_type=f32)
    field = both[: 2 * height] + both[2 * height :]
    field += jnp.dot(table_hi, modes_lo, preferred_element_type=f32)
    even, odd = field[:height], field[height:]
    sides = [slice(side, side + lanes) for side in (0, lanes)]
    field = [even[:, side] + pltpu.roll(odd[:, side], lanes - per_row, axis=1) for side in sides]
    below_it = jnp.zeros((lanes - height, lanes), f32)
    field = [jnp.concatenate([side, below_it], axis=0).T for side in field]
    starts = [(k // 2, k % 2 * pair) for k in range(4)]
    inc = [
        [field[side][at + c * level_count : at + (c + 1) * level_count] for c in range(3)]
        for side, at in starts
    ]
    padded[...] = jnp.zeros_like(padded)
    x_even = lax.axis_index("ky") % 2 == 0
    y_even = lax.axis_index("gz") % 2 == 0
    inner = slice(1, y_tile + 1)
    padded[0, :, inner] = jnp.where(x_even, x_out[1], x_in[1])
    padded[3, :, inner] = jnp.where(x_even, x_in[0], x_out[0])
    for x in range(2):
        padded[x + 1, :, inner] = comp[x]
        padded[x + 1, :, 0:1] = jnp.where(y_even, y_out[x], y_in[x])[:, y_tile - 1 : y_tile]
        padded[x + 1, :, y_tile + 1 : y_tile + 2] = jnp.where(y_even, y_in[x], y_out[x])[:, 0:1]
    cells = [[padded[k, c * level_count : (c + 1) * level_count] for c in range(3)] for k in range(4)]
    level = lax.broadcasted_iota(jnp.int32, (level_count, lanes), 0)

    def below(v):
        return jnp.where(level == 0, 0.0, pltpu.roll(v, 1, axis=0))

    def above(v):
        return jnp.where(level == level_count - 1, 0.0, pltpu.roll(v, level_count - 1, axis=0))

    def before(v):
        return pltpu.roll(v, 1, axis=1)

    def after(v):
        return pltpu.roll(v, lanes - 1, axis=1)

    x_flux = [flux(face(inc[k], inc[k + 1]), face(cells[k], cells[k + 1]), 0) for k in range(3)]
    for x in range(2):
        own_inc, own = inc[x + 1], cells[x + 1]
        inc_before, own_before = [before(v) for v in own_inc], [before(v) for v in own]
        y_lower = flux(face(inc_before, own_inc), face(own_before, own), 1)
        inc_below, own_below = [below(v) for v in own_inc], [below(v) for v in own]
        inc_above, own_above = [above(v) for v in own_inc], [above(v) for v in own]
        z_lower = flux(face(inc_below, own_inc), face(own_below, own), 2)
        z_upper = flux(face(own_inc, inc_above), face(own, own_above), 2)
        for c in range(3):
            twice = 2.0 * own[c]
            tendency = -(x_flux[x + 1][c] - x_flux[x][c])
            tendency += viscosity * (cells[x][c] + cells[x + 2][c] - twice)
            tendency -= after(y_lower[c]) - y_lower[c]
            tendency += viscosity * (own_before[c] + after(own[c]) - twice)
            tendency -= (z_upper[c] - z_lower[c]) / cell_height
            tendency += viscosity * (own_below[c] + own_above[c] - twice) / cell_height**2
            result = own[c] + time_step * tendency
            incident[x, c] = own_inc[c][:, 1 : y_tile + 1]
            predicted[x, c] = result[:, 1 : y_tile + 1]


def swaps(size, first):
    pairs = [(i, i + 1) for i in range(first, size - 1, 2)]
    return pairs + [(j, i) for i, j in pairs]


PAIRS = (("ky", 0), ("ky", 1), ("gz", 0), ("gz", 1))
ORDER = (("gz", 1), ("gz", 0), ("ky", 1), ("ky", 0))


def on_device(amplitudes, complementary):
    x_tile, level_count, _, y_tile = complementary.shape
    ky_groups, gz_groups = lax.axis_size("ky"), lax.axis_size("gz")
    wave_local, kx_count = amplitudes.shape[1:]
    wave_count = wave_local * ky_groups
    height = -(-(y_tile + 2) // 16) * 16
    chunk = 4 * 2 * wave_local * 3 * level_count // lanes
    vmem = pl.BlockSpec(memory_space=pltpu.VMEM)
    anywhere = pl.BlockSpec(memory_space=pl.ANY)

    def x_call(*refs):
        x_kernel(ky_groups, level_count, wave_count, *refs)

    def y_call(*refs):
        y_kernel(ky_groups, wave_local, height, *refs)

    comp = jnp.transpose(complementary, (0, 2, 1, 3)).reshape(x_tile, 3 * level_count, y_tile)
    with jax.named_scope("x_transform"):
        sent = pl.pallas_call(
            x_call,
            out_shape=jax.ShapeDtypeStruct((ky_groups * chunk, lanes), f32),
            in_specs=[anywhere],
            out_specs=vmem,
            scratch_shapes=[
                pltpu.VMEM(amplitudes.shape, f32),
                pltpu.SemaphoreType.DMA((4,)),
            ],
            name="x_transform",
        )(amplitudes)
    halos = [
        lax.ppermute(comp, axis, swaps(lax.axis_size(axis), first)) for axis, first in ORDER
    ]
    x_in, x_out, y_in, y_out = (halos[ORDER.index(which)] for which in PAIRS)
    order = [*range(ky_groups // 2 - 1, -1, -1), *range(ky_groups // 2, ky_groups)]
    sent = sent.reshape(ky_groups, 1, chunk * lanes)
    received = lax.all_to_all(sent, "ky", 0, 0, axis_index_groups=[order])
    result = jax.ShapeDtypeStruct((x_tile, 3, level_count, y_tile), f32)
    with jax.named_scope("y_transform_and_step"):
        incident, predicted = pl.pallas_call(
            y_call,
            out_shape=(result, result),
            in_specs=[vmem] * 6,
            out_specs=(vmem, vmem),
            scratch_shapes=[pltpu.VMEM((4, 3 * level_count, lanes), f32)],
            compiler_params=pltpu.CompilerParams(vmem_limit_bytes=48 * 2**20),
            name="y_transform",
        )(received.reshape(ky_groups * chunk, lanes), comp, y_out, y_in, x_out, x_in)
    back = (0, 2, 1, 3)
    return jnp.transpose(incident, back), jnp.transpose(predicted, back)


def solution(mesh):
    placed = (P(None, "ky", None), P("ky", None, None, "gz"))
    return jax.shard_map(
        on_device,
        mesh=mesh,
        in_specs=placed,
        out_specs=(P("ky", None, None, "gz"), P("ky", None, None, "gz")),
        check_vma=False,
    )
```
